32 devices in a mesh: groups: 2 (over x), wide: 16 (over z, y, core).
Axes of the slice: x: 2, y: 2, z: 4, core: 2. Of those that a mesh axis runs over, the one named last changes fastest.
Arguments:
- plus_counts: int32 [8192, 8, 2048], P(('groups', 'wide')), parts along dimension 0, may hold values from 32 to 160
- report_counts: int32 [8192, 8, 2048], P(('groups', 'wide')), parts along dimension 0, may hold values from 128 to 256
- clip_bounds: int32 [8192, 8], P(('groups', 'wide')), parts along dimension 0, may hold values from 16 to 159
Outputs:
- histogram: float32 [8192, 8, 2048], P(('groups', 'wide')), parts along dimension 0
The draws below stay inside these ranges and needn't reach their ends.
There are 2 independent parts, one for each index of `groups`. The reference program is written for one: setup_inputs(seed, part) draws one part's arguments, and reference() takes and returns one part's arrays. A program takes and returns all parts, laid end to end along the dimension named above; each array names one. Nothing has to cross between parts.
All inputs are finite; a program needn't handle non-finite values.
Results may differ from the reference program's by a relative error of at most 0.0041.
Values may be sent and summed in bfloat16 or wider, within the bound.
A program may use at most 320 MiB of HBM per device.

```python
import jax
import jax.numpy as jnp
from jax import lax

A = 4096
C = 8
B = 2048


def set_ends(entries, key, least, top_value):
    longest = entries.shape.index(max(entries.shape))
    spots = []
    for shift in (0, 1):
        where = [jax.random.randint(jax.random.fold_in(key, axis), (), 0, length) for axis, length in enumerate(entries.shape)]
        where[longest] = (where[longest] + shift) % entries.shape[longest]
        spots.append(tuple(where))
    return entries.at[spots[0]].set(least).at[spots[1]].set(top_value)


def setup_inputs(seed: int = 0, part: int = 0) -> dict:
    keys = jax.random.split(jax.random.key(seed), 4)
    own_keys = jax.random.split(jax.random.fold_in(keys[3], part), 4)
    plus_counts = set_ends(jax.random.randint(own_keys[0], (A, C, B), 32, 161), jax.random.fold_in(own_keys[0], 1), 32, 160).astype(jnp.int32)
    report_counts = set_ends(jax.random.randint(own_keys[1], (A, C, B), 128, 257), jax.random.fold_in(own_keys[1], 1), 128, 256).astype(jnp.int32)
    clip_bounds = set_ends(jax.random.randint(own_keys[2], (A, C), 16, 160), jax.random.fold_in(own_keys[2], 1), 16, 159).astype(jnp.int32)
    return {"plus_counts": plus_counts, "report_counts": report_counts, "clip_bounds": clip_bounds}


def sylvester(order):
    idx = jnp.arange(order, dtype=jnp.int32)
    both = jnp.bitwise_and(idx[:, None], idx[None, :])
    parity = jnp.zeros((order, order), jnp.int32)
    for shift_bit in range(max(order.bit_length() - 1, 1)):
        parity = parity + jnp.bitwise_and(jnp.right_shift(both, shift_bit), 1)
    return (1.0 - 2.0 * jnp.bitwise_and(parity, 1).astype(jnp.float32)).astype(jnp.float32)


def kron_hadamard(order):
    left_order = 64 if order >= 4096 else max(order // 64, 1)
    right_order = order // left_order
    left = sylvester(left_order).astype(jnp.bfloat16)
    right = sylvester(right_order).astype(jnp.bfloat16)
    return (left[:, None, :, None] * right[None, :, None, :]).reshape(order, order)


def reference(plus_counts, report_counts, clip_bounds):
    bound = clip_bounds[:, :, None]
    numer = jnp.clip(2 * plus_counts - report_counts, -bound, bound).astype(jnp.float32)
    residual = (numer / report_counts.astype(jnp.float32)).astype(jnp.bfloat16)
    hadamard_b = kron_hadamard(B)
    hadamard_c = sylvester(C)
    hadamard_a = kron_hadamard(A)
    inner = jnp.dot(residual.reshape(A * C, B), hadamard_b, preferred_element_type=jnp.float32).reshape(A, C, B)
    inner = jnp.einsum("dc,acb->adb", hadamard_c, inner, precision=lax.Precision.HIGHEST)
    mixed = (inner * (1.0 / 128.0)).astype(jnp.bfloat16)
    outer = jnp.dot(hadamard_a, mixed.reshape(A, C * B), preferred_element_type=jnp.float32)
    return (outer * (1.0 / 64.0)).reshape(A, C, B)
```

```python
import functools

import jax
import jax.numpy as jnp
from jax import lax
from jax.experimental import pallas as pl
from jax.experimental.pallas import tpu as pltpu
from jax.sharding import PartitionSpec as P

CHUNK = 32
PAIR = 2
FACTOR = 256
LANES = 128
RADIX = 16
MESH = pl.DeviceIdType.MESH


def butterfly(parts):
    parts = list(parts)
    half = 1
    while half < len(parts):
        for low in range(len(parts)):
            if not low & half:
                first, second = parts[low], parts[low | half]
                parts[low], parts[low | half] = first + second, first - second
        half *= 2
    return parts


def signs(both):
    for shift in (8, 4, 2, 1):
        both = both ^ (both >> shift)
    return (1 - 2 * (both & 1)).astype(jnp.float32)


def exchange(
    n, plus_ref, report_ref, bound_ref, out_ref,
    had_b, had_c, plus_buf, report_buf, inner, mixed, got, summed,
    load_sem, send_one, recv_one, send_two, recv_two, own_sem,
):
    me = lax.axis_index("wide")
    chunks, tall, trailing = plus_ref.shape
    middle = tall // CHUNK
    per_group, width = mixed.shape[2], mixed.shape[4]
    blocks = trailing // FACTOR

    def loads(k):
        slot = lax.rem(k, 2)
        return (
            pltpu.make_async_copy(plus_ref.at[k], plus_buf.at[slot], load_sem.at[0, slot]),
            pltpu.make_async_copy(report_ref.at[k], report_buf.at[slot], load_sem.at[1, slot]),
        )

    for load in loads(0):
        load.start()

    barrier = pltpu.get_barrier_semaphore()

    def greet(step, carry):
        pl.semaphore_signal(barrier, inc=1, device_id={"wide": lax.rem(me + step, n)}, device_id_type=MESH)
        return carry

    lax.fori_loop(1, n, greet, 0)

    row = lax.broadcasted_iota(jnp.int32, (FACTOR, FACTOR), 0)
    col = lax.broadcasted_iota(jnp.int32, (FACTOR, FACTOR), 1)
    had_b[...] = signs(row & col).astype(jnp.bfloat16)
    row = lax.broadcasted_iota(jnp.int32, (tall, tall), 0)
    col = lax.broadcasted_iota(jnp.int32, (tall, tall), 1)
    near = (row ^ col) < middle
    had_c[...] = jnp.where(near, signs(row & col & (middle - 1)), 0.0).astype(jnp.bfloat16)

    pl.semaphore_wait(barrier, n - 1)

    def front(k, carry):
        slot = lax.rem(k, 2)

        @pl.when(k + 1 < chunks)
        def _():
            for load in loads(k + 1):
                load.start()

        for load in loads(k):
            load.wait()
        bounds = bound_ref[pl.ds(pl.multiple_of(k * CHUNK, CHUNK), CHUNK), :]
        bounds = jnp.broadcast_to(bounds[:, None, :], (CHUNK, middle, middle)).reshape(tall, middle)
        pick = lax.broadcasted_iota(jnp.int32, (tall, middle), 0) % middle
        pick = pick == lax.broadcasted_iota(jnp.int32, (tall, middle), 1)
        bound = jnp.sum(jnp.where(pick, bounds.astype(jnp.float32), 0.0), axis=1, keepdims=True)
        for block in range(blocks):
            cols = pl.ds(block * FACTOR, FACTOR)
            plus = plus_buf[slot, :, cols]
            report = report_buf[slot, :, cols]
            numer = jnp.clip((2 * plus - report).astype(jnp.float32), -bound, bound)
            residual = (numer / report.astype(jnp.float32)).astype(jnp.bfloat16)
            inner[:, cols] = jnp.dot(residual, had_b[...], preferred_element_type=jnp.float32)

        def across(strip, carry):
            rows = pl.ds(pl.multiple_of(strip * 8, 8), 8)
            parts = butterfly([inner[rows, pl.ds(b * FACTOR, FACTOR)] for b in range(blocks)])
            for b in range(blocks):
                inner[rows, pl.ds(b * FACTOR, FACTOR)] = parts[b]
            return carry

        lax.fori_loop(0, tall // 8, across, 0)
        for block in range(blocks):
            whole = inner[:, pl.ds(block * FACTOR, FACTOR)]
            high = whole.astype(jnp.bfloat16)
            low = (whole - high.astype(jnp.float32)).astype(jnp.bfloat16)
            done = jnp.dot(had_c[...], high, preferred_element_type=jnp.float32)
            done = done + jnp.dot(had_c[...], low, preferred_element_type=jnp.float32)
            done = (done * (1.0 / 128.0)).astype(jnp.bfloat16)
            part, start = divmod(block * FACTOR, width)
            mixed[k, :, part, :, pl.ds(start, FACTOR)] = done.reshape(-1, PAIR * middle, FACTOR)
        got[k, 0] = mixed[k, lax.div(me, per_group), lax.rem(me, per_group)]

        def send(step, carry):
            to = lax.rem(me + step, n)
            pltpu.make_async_remote_copy(
                src_ref=mixed.at[k, lax.div(to, per_group), lax.rem(to, per_group)],
                dst_ref=got.at[k, step],
                send_sem=send_one.at[k],
                recv_sem=recv_one.at[k],
                device_id={"wide": to},
                device_id_type=MESH,
            ).start()
            return carry

        lax.fori_loop(1, n, send, 0)
        return carry

    lax.fori_loop(0, chunks, front, 0)

    def wait_all(k, sem):
        others = got.at[k, pl.ds(1, n - 1)]
        pltpu.make_async_copy(others, others, sem.at[k]).wait()

    def own(k):
        return pltpu.make_async_copy(
            summed.at[k, me], out_ref.at[k, lax.div(me, per_group), lax.rem(me, per_group)], own_sem.at[k]
        )

    def combine(k, carry):
        wait_all(k, recv_one)

        def strip(tile, carry):
            cols = pl.ds(pl.multiple_of(tile * LANES, LANES), LANES)
            parts = [got[k, lax.rem(me + (n - source), n), :, cols].astype(jnp.float32) for source in range(n)]
            parts = butterfly(parts)
            for to in range(n):
                summed[k, to, :, cols] = (parts[to] * (1.0 / 64.0)).astype(jnp.bfloat16)
            return carry

        lax.fori_loop(0, width // LANES, strip, 0)
        own(k).start()

        def send(step, carry):
            to = lax.rem(me + step, n)
            pltpu.make_async_remote_copy(
                src_ref=summed.at[k, to],
                dst_ref=out_ref.at[k, lax.div(me, per_group), lax.rem(me, per_group)],
                send_sem=send_two.at[k],
                recv_sem=recv_two.at[k],
                device_id={"wide": to},
                device_id_type=MESH,
            ).start()
            return carry

        lax.fori_loop(1, n, send, 0)
        return carry

    lax.fori_loop(0, chunks, combine, 0)

    def finish(k, carry):
        own(k).wait()
        wait_all(k, send_one)
        wait_all(k, send_two)
        wait_all(k, recv_two)
        return carry

    lax.fori_loop(0, chunks, finish, 0)


def leading(summed_ref, out_ref):
    rows, middle, wide = out_ref.shape
    chunks, groups = summed_ref.shape[:2]
    tiles = wide // LANES
    per_chunk = CHUNK // RADIX

    def inside(index, carry):
        block, tile = index // tiles, index % tiles
        cols = pl.ds(pl.multiple_of(tile * LANES, LANES), LANES)
        group = pl.ds((block % per_chunk) * (RADIX // PAIR), RADIX // PAIR)
        parts = summed_ref[block // per_chunk, group, 0, :, cols].astype(jnp.float32)
        parts = parts.reshape(RADIX, middle, LANES)
        parts = butterfly([parts[i] for i in range(RADIX)])
        for i in range(RADIX):
            out_ref[block * RADIX + i, :, cols] = parts[i]
        return carry

    lax.fori_loop(0, rows // RADIX * tiles, inside, 0)

    def across(index, carry):
        low, tile = index // tiles, index % tiles
        cols = pl.ds(pl.multiple_of(tile * LANES, LANES), LANES)
        parts = butterfly([out_ref[high * RADIX + low, :, cols] for high in range(rows // RADIX)])
        for high in range(rows // RADIX):
            out_ref[high * RADIX + low, :, cols] = parts[high]
        return carry

    lax.fori_loop(0, RADIX * tiles, across, 0)


def shards(plus_counts, report_counts, clip_bounds):
    rows, middle, trailing = plus_counts.shape
    n = lax.axis_size("wide")
    chunks, tall = rows // CHUNK, CHUNK * middle
    groups = CHUNK // PAIR
    per_group = n // groups
    width = trailing // per_group
    piece = (PAIR * middle, width)
    summed = pl.pallas_call(
        functools.partial(exchange, n),
        out_shape=jax.ShapeDtypeStruct((chunks, groups, per_group) + piece, jnp.bfloat16),
        in_specs=[
            pl.BlockSpec(memory_space=pl.ANY),
            pl.BlockSpec(memory_space=pl.ANY),
            pl.BlockSpec(memory_space=pltpu.VMEM),
        ],
        out_specs=pl.BlockSpec(memory_space=pl.ANY),
        scratch_shapes=[
            pltpu.VMEM((FACTOR, FACTOR), jnp.bfloat16),
            pltpu.VMEM((tall, tall), jnp.bfloat16),
            pltpu.VMEM((2, tall, trailing), jnp.int32),
            pltpu.VMEM((2, tall, trailing), jnp.int32),
            pltpu.VMEM((tall, trailing), jnp.float32),
            pltpu.VMEM((chunks, groups, per_group) + piece, jnp.bfloat16),
            pltpu.VMEM((chunks, n) + piece, jnp.bfloat16),
            pltpu.VMEM((chunks, n) + piece, jnp.bfloat16),
            pltpu.SemaphoreType.DMA((2, 2)),
            pltpu.SemaphoreType.DMA((chunks,)),
            pltpu.SemaphoreType.DMA((chunks,)),
            pltpu.SemaphoreType.DMA((chunks,)),
            pltpu.SemaphoreType.DMA((chunks,)),
            pltpu.SemaphoreType.DMA((chunks,)),
        ],
        compiler_params=pltpu.CompilerParams(
            collective_id=0, has_side_effects=True, vmem_limit_bytes=56 * 1024 * 1024
        ),
    )(
        plus_counts.reshape(chunks, tall, trailing),
        report_counts.reshape(chunks, tall, trailing),
        clip_bounds,
    )
    wide = 256
    inside = width // wide
    return pl.pallas_call(
        leading,
        grid=(trailing // wide,),
        out_shape=jax.ShapeDtypeStruct((rows, middle, trailing), jnp.float32),
        in_specs=[
            pl.BlockSpec((chunks, groups, 1, PAIR * middle, wide), lambda c: (0, 0, c // inside, 0, c % inside))
        ],
        out_specs=pl.BlockSpec((rows, middle, wide), lambda c: (0, 0, c)),
        compiler_params=pltpu.CompilerParams(vmem_limit_bytes=32 * 1024 * 1024),
    )(summed)


def solution(mesh):
    placed = (
        P(("groups", "wide"), None, None),
        P(("groups", "wide"), None, None),
        P(("groups", "wide"), None),
    )
    return jax.shard_map(
        shards,
        mesh=mesh,
        in_specs=placed,
        out_specs=P(("groups", "wide"), None, None),
        check_vma=False,
    )
```

```python
import functools

import jax
import jax.numpy as jnp
from jax import lax
from jax.experimental import pallas as pl
from jax.experimental.pallas import tpu as pltpu
from jax.sharding import PartitionSpec as P

CHUNK = 32
PAIR = 2
FACTOR = 256
LANES = 128
RADIX = 16
MESH = pl.DeviceIdType.MESH


def butterfly(parts):
    parts = list(parts)
    half = 1
    while half < len(parts):
        for low in range(len(parts)):
            if not low & half:
                first, second = parts[low], parts[low | half]
                parts[low], parts[low | half] = first + second, first - second
        half *= 2
    return parts


def signs(both):
    for shift in (8, 4, 2, 1):
        both = both ^ (both >> shift)
    return (1 - 2 * (both & 1)).astype(jnp.float32)


def order(turn, n):
    later = lax.rem(turn, 2)
    return n - 1 - lax.div(turn, 2) - later * (n // 2)


def partner(me, other, n):
    bit, found = 1, 0
    while bit < n:
        found = found + lax.rem(lax.div(me, bit) + (other // bit), 2) * bit
        bit *= 2
    return found


def exchange(
    n, plus_ref, report_ref, bound_ref, out_ref,
    had_b, had_c, bounds, plus_buf, report_buf, inner, mixed, got, summed,
    load_sem, send_one, recv_one, send_two, recv_two, own_sem,
):
    me = lax.axis_index("wide")
    chunks, tall, trailing = plus_ref.shape
    middle = tall // CHUNK
    per_group, width = mixed.shape[2], mixed.shape[4]
    blocks = trailing // FACTOR

    def loads(k):
        slot = lax.rem(k, 2)
        return (
            pltpu.make_async_copy(plus_ref.at[k], plus_buf.at[slot], load_sem.at[0, slot]),
            pltpu.make_async_copy(report_ref.at[k], report_buf.at[slot], load_sem.at[1, slot]),
        )

    for load in loads(0):
        load.start()

    barrier = pltpu.get_barrier_semaphore()

    def greet(step, carry):
        pl.semaphore_signal(barrier, inc=1, device_id={"wide": lax.rem(me + step, n)}, device_id_type=MESH)
        return carry

    lax.fori_loop(1, n, greet, 0)

    row = lax.broadcasted_iota(jnp.int32, (FACTOR, FACTOR), 0)
    col = lax.broadcasted_iota(jnp.int32, (FACTOR, FACTOR), 1)
    had_b[...] = signs(row & col).astype(jnp.bfloat16)
    row = lax.broadcasted_iota(jnp.int32, (tall, tall), 0)
    col = lax.broadcasted_iota(jnp.int32, (tall, tall), 1)
    had_c[...] = signs(row & col).astype(jnp.bfloat16)
    turned = (row == col).astype(jnp.float32).astype(jnp.bfloat16)
    for k in range(chunks):
        part = bound_ref[...] if chunks == 1 else bound_ref[:, k * CHUNK : (k + 1) * CHUNK]
        bounds[pl.ds(k * CHUNK, CHUNK), :] = lax.dot_general(
            turned[:CHUNK, :CHUNK], part.astype(jnp.float32).astype(jnp.bfloat16),
            (((1,), (1,)), ((), ())), preferred_element_type=jnp.float32)

    pl.semaphore_wait(barrier, n - 1)

    def front(k, carry):
        slot = lax.rem(k, 2)

        @pl.when(k + 1 < chunks)
        def _():
            for load in loads(k + 1):
                load.start()

        for load in loads(k):
            load.wait()
        each = bounds[pl.ds(pl.multiple_of(k * CHUNK, CHUNK), CHUNK), :]
        each = jnp.broadcast_to(each[:, None, :], (CHUNK, middle, middle)).reshape(tall, middle)
        pick = lax.broadcasted_iota(jnp.int32, (tall, middle), 0) % middle
        pick = pick == lax.broadcasted_iota(jnp.int32, (tall, middle), 1)
        bound = jnp.sum(jnp.where(pick, each, 0.0), axis=1, keepdims=True)
        for block in range(blocks):
            cols = pl.ds(block * FACTOR, FACTOR)
            plus = plus_buf[slot, :, cols]
            report = report_buf[slot, :, cols]
            numer = jnp.clip((2 * plus - report).astype(jnp.float32), -bound, bound)
            residual = (numer / report.astype(jnp.float32)).astype(jnp.bfloat16)
            inner[:, cols] = jnp.dot(residual, had_b[...], preferred_element_type=jnp.float32)

        def across(strip, carry):
            rows = pl.ds(pl.multiple_of(strip * 8, 8), 8)
            parts = butterfly([inner[rows, pl.ds(b * FACTOR, FACTOR)] for b in range(blocks)])
            for b in range(blocks):
                inner[rows, pl.ds(b * FACTOR, FACTOR)] = parts[b]
            return carry

        lax.fori_loop(0, tall // 8, across, 0)
        for block in range(blocks):
            whole = inner[:, pl.ds(block * FACTOR, FACTOR)]
            high = whole.astype(jnp.bfloat16)
            low = (whole - high.astype(jnp.float32)).astype(jnp.bfloat16)
            done = jnp.dot(had_c[...], high, preferred_element_type=jnp.float32)
            done = done + jnp.dot(had_c[...], low, preferred_element_type=jnp.float32)
            done = (done * (1.0 / 128.0)).astype(jnp.bfloat16)
            part, start = divmod(block * FACTOR, width)
            mixed[k, :, part, :, pl.ds(start, FACTOR)] = done.reshape(-1, PAIR * middle, FACTOR)
        got[k, 0] = mixed[k, lax.div(me, per_group), lax.rem(me, per_group)]

        def send(turn, carry):
            step = order(turn, n)
            to = partner(me, step, n)
            pltpu.make_async_remote_copy(
                src_ref=mixed.at[k, lax.div(to, per_group), lax.rem(to, per_group)],
                dst_ref=got.at[k, step],
                send_sem=send_one.at[k],
                recv_sem=recv_one.at[k],
                device_id={"wide": to},
                device_id_type=MESH,
            ).start()
            return carry

        lax.fori_loop(0, n - 1, send, 0)
        return carry

    lax.fori_loop(0, chunks, front, 0)

    def wait_all(k, sem):
        others = got.at[k, pl.ds(1, n - 1)]
        pltpu.make_async_copy(others, others, sem.at[k]).wait()

    def own(k):
        return pltpu.make_async_copy(
            summed.at[k, me], out_ref.at[k, lax.div(me, per_group), lax.rem(me, per_group)], own_sem.at[k]
        )

    def combine(k, carry):
        wait_all(k, recv_one)

        def strip(tile, carry):
            cols = pl.ds(pl.multiple_of(tile * LANES, LANES), LANES)
            parts = [got[k, partner(me, source, n), :, cols].astype(jnp.float32) for source in range(n)]
            parts = butterfly(parts)
            for to in range(n):
                summed[k, to, :, cols] = (parts[to] * (1.0 / 64.0)).astype(jnp.bfloat16)
            return carry

        lax.fori_loop(0, width // LANES, strip, 0)
        own(k).start()

        def send(turn, carry):
            step = order(turn, n)
            to = partner(me, step, n)
            pltpu.make_async_remote_copy(
                src_ref=summed.at[k, to],
                dst_ref=out_ref.at[k, lax.div(me, per_group), lax.rem(me, per_group)],
                send_sem=send_two.at[k],
                recv_sem=recv_two.at[k],
                device_id={"wide": to},
                device_id_type=MESH,
            ).start()
            return carry

        lax.fori_loop(0, n - 1, send, 0)
        return carry

    lax.fori_loop(0, chunks, combine, 0)

    def finish(k, carry):
        own(k).wait()
        wait_all(k, send_one)
        wait_all(k, send_two)
        wait_all(k, recv_two)
        return carry

    lax.fori_loop(0, chunks, finish, 0)


def leading(summed_ref, out_ref):
    rows, middle, wide = out_ref.shape
    chunks, groups = summed_ref.shape[:2]

    def inside(group, carry):
        for tile in range(wide // LANES):
            cols = pl.ds(tile * LANES, LANES)
            parts = butterfly([summed_ref[k, group, 0, :, cols].astype(jnp.float32) for k in range(chunks)])
            for k in range(chunks):
                out_ref[pl.ds(k * CHUNK + group * PAIR, PAIR), :, cols] = parts[k].reshape(PAIR, middle, LANES)
        return carry

    lax.fori_loop(0, groups, inside, 0)


def shards(plus_counts, report_counts, clip_bounds):
    rows, middle, trailing = plus_counts.shape
    n = lax.axis_size("wide")
    chunks, tall = rows // CHUNK, CHUNK * middle
    groups = CHUNK // PAIR
    per_group = n // groups
    width = trailing // per_group
    piece = (PAIR * middle, width)
    summed = pl.pallas_call(
        functools.partial(exchange, n),
        out_shape=jax.ShapeDtypeStruct((chunks, groups, per_group) + piece, jnp.bfloat16),
        in_specs=[
            pl.BlockSpec(memory_space=pl.ANY),
            pl.BlockSpec(memory_space=pl.ANY),
            pl.BlockSpec(memory_space=pltpu.VMEM),
        ],
        out_specs=pl.BlockSpec(memory_space=pl.ANY),
        scratch_shapes=[
            pltpu.VMEM((FACTOR, FACTOR), jnp.bfloat16),
            pltpu.VMEM((tall, tall), jnp.bfloat16),
            pltpu.VMEM((rows, middle), jnp.float32),
            pltpu.VMEM((2, tall, trailing), jnp.int32),
            pltpu.VMEM((2, tall, trailing), jnp.int32),
            pltpu.VMEM((tall, trailing), jnp.float32),
            pltpu.VMEM((chunks, groups, per_group) + piece, jnp.bfloat16),
            pltpu.VMEM((chunks, n) + piece, jnp.bfloat16),
            pltpu.VMEM((chunks, n) + piece, jnp.bfloat16),
            pltpu.SemaphoreType.DMA((2, 2)),
            pltpu.SemaphoreType.DMA((chunks,)),
            pltpu.SemaphoreType.DMA((chunks,)),
            pltpu.SemaphoreType.DMA((chunks,)),
            pltpu.SemaphoreType.DMA((chunks,)),
            pltpu.SemaphoreType.DMA((chunks,)),
        ],
        compiler_params=pltpu.CompilerParams(
            collective_id=0, has_side_effects=True, vmem_limit_bytes=42 * 1024 * 1024
        ),
    )(
        plus_counts.reshape(chunks, tall, trailing),
        report_counts.reshape(chunks, tall, trailing),
        clip_bounds.T,
    )
    wide = 256
    inside = width // wide
    return pl.pallas_call(
        leading,
        grid=(trailing // wide,),
        out_shape=jax.ShapeDtypeStruct((rows, middle, trailing), jnp.float32),
        in_specs=[
            pl.BlockSpec((chunks, groups, 1, PAIR * middle, wide), lambda c: (0, 0, c // inside, 0, c % inside))
        ],
        out_specs=pl.BlockSpec((rows, middle, wide), lambda c: (0, 0, c)),
        compiler_params=pltpu.CompilerParams(vmem_limit_bytes=42 * 1024 * 1024),
    )(summed)


def solution(mesh):
    placed = (
        P(("groups", "wide"), None, None),
        P(("groups", "wide"), None, None),
        P(("groups", "wide"), None),
    )
    return jax.shard_map(
        shards,
        mesh=mesh,
        in_specs=placed,
        out_specs=P(("groups", "wide"), None, None),
        check_vma=False,
    )
```
